32 devices in a mesh: dp: 16 (over z, y, x), tensor: 2 (over core).
Axes of the slice: x: 2, y: 2, z: 4, core: 2. Of those that a mesh axis runs over, the one named last changes fastest.
Arguments:
- normed: bfloat16 [8192, 8192], P('dp'), may hold values from -12 to 12
- key_cot: bfloat16 [8192, 256], P('dp', 'tensor'), may hold values from -6 to 6
- key_weight: bfloat16 [8192, 256], P(None, 'tensor'), may hold values from -0.0625 to 0.0625
- norm_gain: bfloat16 [8192], replicated, may hold values from 0.5 to 1.5
- weight_master: float32 [8192, 256], P('dp', 'tensor'), may hold values from -0.0625 to 0.0625
- weight_moment: float32 [8192, 256], P('dp', 'tensor'), may hold values from -0.0041432036 to 0.0041432036
- weight_second: float32 [8192, 256], P('dp', 'tensor'), may hold values from 9.536743e-08 to 2.3841858e-06
- gain_master: float32 [8192], P('dp'), may hold values from 0.5 to 1.5
- gain_moment: float32 [8192], P('dp'), may hold values from -0.0041432036 to 0.0041432036
- gain_second: float32 [8192], P('dp'), may hold values from 9.536743e-08 to 2.3841858e-06
- next_input: bfloat16 [1024, 8192], P('dp'), may hold values from -6 to 6
Outputs:
- next_keys: bfloat16 [1024, 256], P('dp', 'tensor')
- weight_master_new: float32 [8192, 256], P('dp', 'tensor')
- weight_moment_new: float32 [8192, 256], P('dp', 'tensor')
- weight_second_new: float32 [8192, 256], P('dp', 'tensor')
- gain_master_new: float32 [8192], P('dp')
- gain_moment_new: float32 [8192], P('dp')
- gain_second_new: float32 [8192], P('dp')
The draws below stay inside these ranges and needn't reach their ends.
All inputs are finite; a program needn't handle non-finite values.
Results may differ from the reference program's by a relative error of at most 0.001.
The reference program's roundings to bfloat16 on the way (of `scaled` and `next_in`) count: a program that leaves them out, or rounds other values in their place, can miss the bound.
Values may be sent and summed in bfloat16 or wider, within the bound.
A program may use at most 64 MiB of HBM per device.

```python
import math
import jax
import jax.numpy as jnp
from jax import lax

D = 8192
HEAD = 128
TOK = 512
KVH = 2
TOKENS = 8192
NEXT_TOKENS = 1024
N_DP = 16


def draw_normed(key, part):
    base_key = jax.random.fold_in(key, 11)
    pair_key = jax.random.fold_in(key, 23)
    values = jax.random.truncated_normal(base_key, -4.0, 4.0, (TOKENS, D), jnp.float32)
    fall = math.log(6.0)
    column = jnp.arange(D, dtype=jnp.float32)
    column_scale = jnp.exp(-fall * column / (D - 1))
    pairing = jax.random.permutation(pair_key, N_DP)
    token_block = jnp.arange(TOKENS) // TOK
    column_block = jnp.arange(D) // (D // N_DP)
    hit = pairing[token_block][:, None] == column_block[None, :]
    boost = jnp.where(hit, 3.0, 1.0)
    return (values * column_scale[None, :] * boost).astype(jnp.bfloat16)


def shard_levels(rng, dims, cuts, least, high):
    gain, own = 1.0, jax.random.fold_in(rng, 6)
    for position, parts in cuts:
        heights = jnp.exp(jax.random.uniform(jax.random.fold_in(own, position), (parts,), jnp.float32, least / len(cuts), high / len(cuts)))
        gain = gain * jnp.repeat(heights, dims[position] // parts).reshape([-1 if axis == position else 1 for axis in range(len(dims))])
    return gain


def bell_draw(stream_key, extent, deviation, most, split=(), held_as=jnp.bfloat16):
    factor_of = shard_levels(stream_key, extent, split, -0.22, 0.18) if split else 1.0
    entries = jax.random.normal(stream_key, extent, jnp.float32) * deviation * factor_of
    return jnp.minimum(jnp.maximum(entries, -most), most).astype(held_as)


def setup_inputs(seed: int = 0) -> dict:
    seeds = jax.random.split(jax.random.key(seed), 12)
    normed = draw_normed(jax.random.fold_in(seeds[11], 71), 0)
    key_cot = bell_draw(seeds[1], (TOKENS, KVH * HEAD), 1.0, 6.0, ((0, 16), (1, 2)))
    key_weight = bell_draw(seeds[2], (D, KVH * HEAD), D ** -0.5, 0.0625, ((1, 2),))
    norm_gain = jnp.clip(1.0 + 0.1 * jax.random.normal(seeds[3], (D,), jnp.float32), 0.5, 1.5).astype(jnp.bfloat16)
    weight_master = bell_draw(seeds[4], (D, KVH * HEAD), D ** -0.5, 0.0625, ((0, 16), (1, 2)), jnp.float32)
    weight_moment = bell_draw(seeds[5], (D, KVH * HEAD), ((D * HEAD * KVH) ** -0.5), 0.0041432036, ((0, 16), (1, 2)), jnp.float32)
    weight_second = jnp.clip(jnp.exp(math.log(2.384185791015625e-06) - 3.218876 * jax.random.uniform(seeds[6], (D, KVH * HEAD), jnp.float32) ** shard_levels(seeds[6], (D, KVH * HEAD), ((0, 16), (1, 2)), -0.2, 0.2)), 9.536743306171047e-08, 2.384185791015625e-06)
    gain_master = jnp.clip(1.0 + 0.1 * jax.random.normal(seeds[7], (D,), jnp.float32), 0.5, 1.5)
    gain_moment = bell_draw(seeds[8], (D,), ((D * HEAD * KVH) ** -0.5), 0.0041432036, ((0, 16),), jnp.float32)
    gain_second = jnp.clip(jnp.exp(math.log(2.384185791015625e-06) - 3.218876 * jax.random.uniform(seeds[9], (D,), jnp.float32) ** shard_levels(seeds[9], (D,), ((0, 16),), -0.2, 0.2)), 9.536743306171047e-08, 2.384185791015625e-06)
    next_input = bell_draw(seeds[10], (NEXT_TOKENS, D), 1.0, 6.0, ((0, 16),))
    return {"normed": normed, "key_cot": key_cot, "key_weight": key_weight, "norm_gain": norm_gain, "weight_master": weight_master, "weight_moment": weight_moment, "weight_second": weight_second, "gain_master": gain_master, "gain_moment": gain_moment, "gain_second": gain_second, "next_input": next_input}


beta_one = 0.9
beta_two = 0.95
adam_eps = 1e-08
learn_rate = 0.001
rms_eps = 1e-05
step_count = 10

def adam_update(grad, master, moment, second, decay):
    moment_new = beta_one * moment + (1.0 - beta_one) * grad
    second_new = beta_two * second + (1.0 - beta_two) * grad * grad
    corr_one = 1.0 - beta_one ** step_count
    corr_two = 1.0 - beta_two ** step_count
    update = moment_new / corr_one / (jnp.sqrt(second_new / corr_two) + adam_eps) + decay * master
    return (master - learn_rate * update, moment_new, second_new)

def reference(normed, key_cot, key_weight, norm_gain, weight_master, weight_moment, weight_second, gain_master, gain_moment, gain_second, next_input):
    scaled = (normed.astype(jnp.float32) * norm_gain.astype(jnp.float32)[None, :]).astype(jnp.bfloat16)
    key_grad = jnp.dot(scaled.T, key_cot, preferred_element_type=jnp.float32)
    inner = jnp.dot(normed.T, key_cot, preferred_element_type=jnp.float32)
    gain_grad = lax.optimization_barrier(jnp.sum(key_weight.astype(jnp.float32) * inner, axis=1))
    total = jnp.sum(key_grad * key_grad) + jnp.sum(gain_grad * gain_grad)
    clip = jnp.minimum(1.0, 1.0 / (jnp.sqrt(total) + 1e-06))
    weight_new, weight_moment_new, weight_second_new = adam_update(clip * key_grad, weight_master, weight_moment, weight_second, 0.1)
    gain_new, gain_moment_new, gain_second_new = adam_update(clip * gain_grad, gain_master, gain_moment, gain_second, 0.0)
    weight_param = weight_new.astype(jnp.bfloat16)
    gain_param = gain_new.astype(jnp.bfloat16)
    hidden = next_input.astype(jnp.float32)
    inverse = lax.rsqrt(lax.optimization_barrier(jnp.mean(hidden * hidden, axis=1, keepdims=True)) + rms_eps)
    rescaled = hidden * inverse
    next_in = (rescaled * gain_param.astype(jnp.float32)[None, :]).astype(jnp.bfloat16)
    next_keys = jnp.dot(next_in, weight_param, preferred_element_type=jnp.float32).astype(jnp.bfloat16)
    return (next_keys, weight_new, weight_moment_new, weight_second_new, gain_new, gain_moment_new, gain_second_new)
```

```python
import functools

import jax
import jax.numpy as jnp
from jax import lax
from jax.experimental import pallas as pl
from jax.experimental.pallas import tpu as pltpu
from jax.sharding import PartitionSpec as P

beta_one = 0.9
beta_two = 0.95
adam_eps = 1e-08
learn_rate = 0.001
rms_eps = 1e-05
step_count = 10
MESH = pl.DeviceIdType.MESH


def adam_update(grad, master, moment, second, decay):
    moment_new = beta_one * moment + (1.0 - beta_one) * grad
    second_new = beta_two * second + (1.0 - beta_two) * grad * grad
    corr_one = 1.0 - beta_one**step_count
    corr_two = 1.0 - beta_two**step_count
    update = moment_new / corr_one / (jnp.sqrt(second_new / corr_two) + adam_eps) + decay * master
    return (master - learn_rate * update, moment_new, second_new)


def encode(value):
    return (value * jnp.abs(value) * (value * value)).astype(jnp.bfloat16)


def decode(coded):
    power = coded.astype(jnp.float32)
    size = jnp.maximum(jnp.abs(power), 1.2e-38)
    root = lax.rsqrt(size)
    return power * root * lax.rsqrt(size * root)


def kernel(
    dims,
    normed, cot_in, weight_in, gains, gain_in, master_in, moment_in, second_in,
    gmaster, gmoment, gsecond, next_in, next_blocks,
    keys_out, master_out, moment_out, second_out, gmaster_out, gmoment_out, gsecond_out,
    xbuf, cot, kw, master, moment, second, rows_in, prod, got1, give2, got2,
    hbuf, resc, inv_all, gain_all, total_all, part, got_part,
    x_sem, in_sem, own_sem, s1, r1, s2, r2, sh, rh, sm, rm, si, ri, sg, rg, st, rt, sp, rp,
):
    n, heads, q, m, size, width, group, chunks, rows, half_rows = dims
    me = lax.axis_index("dp")
    ten = lax.axis_index("tensor")
    mp = lax.rem(me, q)
    mz = lax.div(me, q)
    half = lax.rem(ten, 2)
    mate = ten + 1 - 2 * half

    def x_copy(c):
        at = pl.ds(pl.multiple_of(c * width, 128), width)
        return pltpu.make_async_copy(normed.at[:, at], xbuf.at[c], x_sem.at[c])

    def loop(low, high, body):
        def step(i, carry):
            body(i)
            return carry

        lax.fori_loop(low, high, step, 0)

    def peer(k):
        return lax.rem(mp + k, q)

    def plane(j):
        return lax.rem(mz + j, m)

    cot_copy = pltpu.make_async_copy(cot_in, cot, in_sem.at[0])
    cot_copy.start()
    if group == 1:

        def fetch(j):
            for k in range(1, q):
                x_copy(plane(j) * q + peer(k)).start()

        loop(1, m + 1, fetch)
        loop(1, m + 1, lambda j: x_copy(plane(j) * q + mp).start())
    else:
        loop(0, chunks, lambda c: x_copy(c).start())
    own_rows = pl.ds(pl.multiple_of(me * size, 16), size)
    local_copies = [
        pltpu.make_async_copy(next_in, rows_in, in_sem.at[1]),
        pltpu.make_async_copy(weight_in.at[own_rows], kw, in_sem.at[2]),
        pltpu.make_async_copy(master_in, master, in_sem.at[3]),
        pltpu.make_async_copy(moment_in, moment, in_sem.at[4]),
        pltpu.make_async_copy(second_in, second, in_sem.at[5]),
    ]
    for copy in local_copies:
        copy.start()

    my_half = pl.ds(pl.multiple_of(half * half_rows, 16), half_rows)

    def next_block(dest):
        if group == 1:
            at = pl.ds(pl.multiple_of(dest * size, 128), size)
            return next_blocks.at[my_half, at]
        return next_blocks.at[dest, my_half]

    own_block = pltpu.make_async_copy(next_block(me), hbuf.at[half, me], own_sem)
    own_block.start()

    barrier = pltpu.get_barrier_semaphore()

    def other(j):
        return lax.rem(me + j, n)

    def greet(j):
        pl.semaphore_signal(barrier, inc=1, device_id=(other(j), ten), device_id_type=MESH)

    loop(1, n, greet)
    for t in range(1, heads):
        pl.semaphore_signal(
            barrier, inc=1, device_id=(me, lax.rem(ten + t, heads)), device_id_type=MESH
        )
    pl.semaphore_wait(barrier, n - 1 + heads - 1)

    def remote(src, dst, send, recv, dev):
        return pltpu.make_async_remote_copy(
            src_ref=src, dst_ref=dst, send_sem=send, recv_sem=recv,
            device_id=dev, device_id_type=MESH,
        )

    def h_copy(j):
        return remote(
            next_block(other(j)), hbuf.at[half, me], sh.at[j], rh.at[j], (other(j), ten)
        )

    loop(1, n, lambda j: h_copy(j).start())

    cot_copy.wait()
    cot_t = cot[...].astype(jnp.float32).T.astype(jnp.bfloat16)

    def product(c):
        x_copy(c).wait()
        scaled = (xbuf[c].astype(jnp.float32) * gains[c]).astype(jnp.bfloat16)
        y = jnp.dot(cot_t, scaled, preferred_element_type=jnp.float32).T
        for g in range(group):
            prod[c * group + g] = encode(y[g * size : (g + 1) * size])

    def copy1(j, k):
        z = plane(j)
        return remote(
            prod.at[z * q + peer(k)], got1.at[(k - 1) * m + z],
            s1.at[(k - 1) * m + z], r1.at[(k - 1) * m + z], (mz * q + peer(k), ten),
        )

    if group > 1:
        loop(0, chunks, product)

    def stage1(j):
        for k in range(1, q):
            if group == 1:
                product(plane(j) * q + peer(k))
            copy1(j, k).start()

    loop(1, m + 1, stage1)

    local_copies[0].wait()
    total_row = jnp.zeros((rows, 128), jnp.float32)
    depth = rows_in.shape[1]
    for at in range(0, depth, 1024):
        piece = rows_in[:, at : at + 1024].astype(jnp.float32)
        piece = piece * piece
        for lane in range(0, 1024, 128):
            total_row = total_row + piece[:, lane : lane + 128]
    inverse = lax.rsqrt(jnp.sum(total_row, axis=1, keepdims=True) / depth + rms_eps)
    square = jnp.broadcast_to(inverse, (rows, 128))
    if rows < 128:
        square = jnp.concatenate([square, jnp.zeros((128 - rows, 128), jnp.float32)], axis=0)
    inv_all[me] = square.T[0:8]

    def i_copy(j):
        return remote(inv_all.at[me], inv_all.at[me], si.at[j], ri.at[j], (other(j), ten))

    loop(1, n, lambda j: i_copy(j).start())

    if group == 1:
        loop(1, m + 1, lambda j: product(plane(j) * q + mp))

    def copy2(j):
        return remote(
            give2.at[j], got2.at[j], s2.at[j], r2.at[j], (plane(j) * q + mp, ten)
        )

    def plane_sum(j):
        total = decode(prod[plane(j) * q + mp])
        for k in range(1, q):
            copy1(j, k).wait_recv()
            total = total + decode(got1[(k - 1) * m + plane(j)])
        return total

    def stage2(j):
        give2[j] = encode(plane_sum(j))
        copy2(j).start()

    loop(1, m, stage2)

    own_block.wait()
    loop(1, n, lambda j: h_copy(j).wait_recv())
    mate_give = remote(hbuf.at[half], hbuf.at[half], sm, rm, (me, mate))
    mate_take = remote(hbuf.at[1 - half], hbuf.at[1 - half], sm, rm, (me, mate))
    mate_give.start()

    key_grad = plane_sum(m)
    for copy in local_copies[1:]:
        copy.wait()
    kw_t = kw[...].astype(jnp.float32).T / gain_in[me]

    loop(1, n, lambda j: i_copy(j).wait_recv())
    mate_take.wait_recv()

    def rescale(s):
        column = jnp.broadcast_to(inv_all[s][0:1], (128, 128)).T[:rows, 0:1]
        for h in range(2):
            at = slice(h * half_rows, (h + 1) * half_rows)
            resc[s, at] = hbuf[h, s].astype(jnp.float32) * column[at]

    loop(0, n, rescale)

    for j in range(1, m):
        copy2(j).wait_recv()
        key_grad = key_grad + decode(got2[j])

    grad_t = key_grad.T
    gain_all[ten, 0:1] = jnp.sum(kw_t * grad_t, axis=0, keepdims=True)
    gain_all[ten, 1:2] = jnp.sum(grad_t * grad_t, axis=0, keepdims=True)

    def g_copy(t):
        dev = (me, lax.rem(ten + t, heads))
        return remote(gain_all.at[ten], gain_all.at[ten], sg.at[t], rg.at[t], dev)

    for t in range(1, heads):
        g_copy(t).start()
    for t in range(1, heads):
        g_copy(t).wait_recv()
    gain_grad = gain_all[0, 0:1]
    squares = gain_all[0, 1:2]
    for t in range(1, heads):
        gain_grad = gain_grad + gain_all[t, 0:1]
        squares = squares + gain_all[t, 1:2]
    squares = squares + gain_grad * gain_grad
    total_all[me] = jnp.broadcast_to(jnp.sum(squares, axis=1, keepdims=True), (8, 128))

    def t_copy(j):
        return remote(total_all.at[me], total_all.at[me], st.at[j], rt.at[j], (other(j), ten))

    loop(1, n, lambda j: t_copy(j).start())
    loop(1, n, lambda j: t_copy(j).wait_recv())
    total = jnp.sum(total_all[...], axis=0)
    clip = jnp.minimum(1.0, 1.0 / (jnp.sqrt(total) + 1e-06))[0:1]

    master_new, moment_new, second_new = adam_update(
        key_grad * clip, master[...], moment[...], second[...], 0.1
    )
    master_out[...] = master_new
    moment_out[...] = moment_new
    second_out[...] = second_new
    weight = master_new.astype(jnp.bfloat16)
    gain_new, gain_moment_new, gain_second_new = adam_update(
        gain_grad * clip[:, 0:1], gmaster[...], gmoment[...], gsecond[...], 0.0
    )
    gmaster_out[...] = gain_new
    gmoment_out[...] = gain_moment_new
    gsecond_out[...] = gain_second_new
    gain = gain_new.astype(jnp.bfloat16).astype(jnp.float32)

    def keys(s):
        mixed = (resc[s] * gain).astype(jnp.bfloat16)
        return jnp.dot(mixed, weight, preferred_element_type=jnp.float32)

    def p_copy(j):
        return remote(part.at[j], got_part.at[j], sp.at[j], rp.at[j], (other(j), ten))

    def share(j):
        part[j] = keys(other(j))
        p_copy(j).start()

    loop(1, n, share)
    part[0] = keys(me)

    def collect(j):
        p_copy(j).wait_recv()
        part[0] = part[0] + got_part[j]

    loop(1, n, collect)
    keys_out[...] = part[0].astype(jnp.bfloat16)

    def drain(j):
        h_copy(j).wait_send()
        i_copy(j).wait_send()
        t_copy(j).wait_send()
        p_copy(j).wait_send()

    loop(1, n, drain)

    def drain1(j):
        for k in range(1, q):
            copy1(j, k).wait_send()

    loop(1, m + 1, drain1)
    loop(1, m, lambda j: copy2(j).wait_send())
    mate_give.wait_send()
    for t in range(1, heads):
        g_copy(t).wait_send()


def local(
    normed,
    key_cot,
    key_weight,
    norm_gain,
    weight_master,
    weight_moment,
    weight_second,
    gain_master,
    gain_moment,
    gain_second,
    next_input,
):
    n = lax.axis_size("dp")
    heads = lax.axis_size("tensor")
    tokens, depth = normed.shape
    size = depth // n
    cols = key_cot.shape[1]
    rows = next_input.shape[0]
    half_rows = rows // 2
    q = 4 if n % 4 == 0 else 1
    m = n // q
    width = size if size % 128 == 0 else 512
    group = width // size
    chunks = depth // width
    dims = (n, heads, q, m, size, width, group, chunks, rows, half_rows)
    if group == 1:
        blocks = next_input
    else:
        blocks = next_input.reshape(rows, n, size).transpose(1, 0, 2)
    gain = norm_gain.astype(jnp.float32)
    hbm = pl.BlockSpec(memory_space=pl.ANY)
    vmem = pl.BlockSpec(memory_space=pltpu.VMEM)
    f32, bf16 = jnp.float32, jnp.bfloat16
    dma = pltpu.SemaphoreType.DMA
    shard = jax.ShapeDtypeStruct((size, cols), f32)
    line = jax.ShapeDtypeStruct((1, size), f32)
    outs = pl.pallas_call(
        functools.partial(kernel, dims),
        out_shape=(
            jax.ShapeDtypeStruct((rows, cols), bf16), shard, shard, shard, line, line, line,
        ),
        in_specs=[hbm, hbm, hbm, vmem, vmem, hbm, hbm, hbm, vmem, vmem, vmem, hbm, hbm],
        out_specs=(vmem,) * 7,
        scratch_shapes=[
            pltpu.VMEM((chunks, tokens, width), bf16),
            pltpu.VMEM((tokens, cols), bf16),
            pltpu.VMEM((size, cols), bf16),
            pltpu.VMEM((size, cols), f32),
            pltpu.VMEM((size, cols), f32),
            pltpu.VMEM((size, cols), f32),
            pltpu.VMEM((rows, depth), bf16),
            pltpu.VMEM((n, size, cols), bf16),
            pltpu.VMEM((max(q - 1, 1) * m, size, cols), bf16),
            pltpu.VMEM((m, size, cols), bf16),
            pltpu.VMEM((m, size, cols), bf16),
            pltpu.VMEM((2, n, half_rows, size), bf16),
            pltpu.VMEM((n, rows, size), f32),
            pltpu.VMEM((n, 8, 128), f32),
            pltpu.VMEM((heads, 8, size), f32),
            pltpu.VMEM((n, 8, 128), f32),
            pltpu.VMEM((n, rows, cols), f32),
            pltpu.VMEM((n, rows, cols), f32),
            dma((chunks,)), dma((6,)), dma,
            dma((max(q - 1, 1) * m,)), dma((max(q - 1, 1) * m,)),
            dma((m,)), dma((m,)),
            dma((n,)), dma((n,)),
            dma, dma,
            dma((n,)), dma((n,)),
            dma((heads,)), dma((heads,)),
            dma((n,)), dma((n,)),
            dma((n,)), dma((n,)),
        ],
        compiler_params=pltpu.CompilerParams(
            collective_id=0, has_side_effects=True, vmem_limit_bytes=52 * 1024 * 1024
        ),
        cost_estimate=pl.CostEstimate(
            flops=2 * tokens * depth * cols + 2 * n * rows * size * cols,
            bytes_accessed=2 * tokens * depth,
            transcendentals=0,
        ),
    )(
        normed, key_cot, key_weight,
        gain.reshape(chunks, 1, width), gain.reshape(n, 1, size), weight_master, weight_moment, weight_second,
        gain_master.reshape(1, size), gain_moment.reshape(1, size),
        gain_second.reshape(1, size), next_input, blocks,
    )
    keys, master, moment, second, gmaster, gmoment, gsecond = outs
    return (
        keys, master, moment, second,
        gmaster.reshape(size), gmoment.reshape(size), gsecond.reshape(size),
    )


def solution(mesh):
    return jax.shard_map(
        local,
        mesh=mesh,
        in_specs=(
            P("dp", None),
            P("dp", "tensor"),
            P(None, "tensor"),
            P(),
            P("dp", "tensor"),
            P("dp", "tensor"),
            P("dp", "tensor"),
            P("dp"),
            P("dp"),
            P("dp"),
            P("dp", None),
        ),
        out_specs=(
            P("dp", "tensor"),
            P("dp", "tensor"),
            P("dp", "tensor"),
            P("dp", "tensor"),
            P("dp"),
            P("dp"),
            P("dp"),
        ),
        check_vma=False,
    )
```

```python
import functools

import jax
import jax.numpy as jnp
from jax import lax
from jax.experimental import pallas as pl
from jax.experimental.pallas import tpu as pltpu
from jax.sharding import PartitionSpec as P

beta_one = 0.9
beta_two = 0.95
adam_eps = 1e-08
learn_rate = 0.001
rms_eps = 1e-05
step_count = 10
MESH = pl.DeviceIdType.MESH


def adam_update(grad, master, moment, second, decay):
    moment_new = beta_one * moment + (1.0 - beta_one) * grad
    second_new = beta_two * second + (1.0 - beta_two) * grad * grad
    corr_one = 1.0 - beta_one**step_count
    corr_two = 1.0 - beta_two**step_count
    update = moment_new / corr_one / (jnp.sqrt(second_new / corr_two) + adam_eps) + decay * master
    return (master - learn_rate * update, moment_new, second_new)


def encode(value):
    return (value * jnp.abs(value) * (value * value)).astype(jnp.bfloat16)


def decode(coded):
    power = coded.astype(jnp.float32)
    size = jnp.maximum(jnp.abs(power), 1.2e-38)
    root = lax.rsqrt(size)
    return power * root * lax.rsqrt(size * root)


def kernel(
    dims,
    normed, cot_in, weight_in, gains_in, gain_in_hbm, master_in, moment_in, second_in,
    gmaster_in, gmoment_in, gsecond_in, next_in, next_blocks,
    keys_out, master_out, moment_out, second_out, gmaster_out, gmoment_out, gsecond_out,
    xbuf, cot, kw, master, moment, second, rows_in, prod, got1, give2, got2,
    hbuf, resc, inv_all, gain_all, total_all, part, got_part, give_keys, got_keys,
    gains, gain_in, gmaster, gmoment, gsecond, keys_v, master_v, moment_v, second_v,
    gmaster_v, gmoment_v, gsecond_v,
    x_sem, in_sem, own_sem, s1, r1, s2, r2, sh, rh, sm, rm, si, ri, sg, rg, st, rt, sp, rp, s3, r3, out_sem,
):
    n, heads, q, m, size, width, group, chunks, rows, half_rows = dims
    me = lax.axis_index("dp")
    ten = lax.axis_index("tensor")
    mp = lax.rem(me, q)
    mz = lax.div(me, q)
    half = lax.rem(ten, 2)
    mate = ten + 1 - 2 * half

    def x_copy(c):
        at = pl.ds(pl.multiple_of(c * width, 128), width)
        return pltpu.make_async_copy(normed.at[:, at], xbuf.at[c], x_sem.at[c])

    def loop(low, high, body):
        def step(i, carry):
            body(i)
            return carry

        lax.fori_loop(low, high, step, 0)

    def peer(k):
        return lax.rem(mp + k, q)

    def plane(j):
        return lax.rem(mz + j, m)

    across = lax.rem(mp, 2)
    along = lax.div(mp, 2)
    in_row = 1 - across + 2 * along
    in_column = across + 2 * (1 - along)
    diagonal = 3 - mp

    def near_one(j):
        return in_column + (in_row - in_column) * lax.rem(j, 2)

    def near_two(j):
        return in_row + (in_column - in_row) * lax.rem(j, 2)

    cot_copy = pltpu.make_async_copy(cot_in, cot, in_sem.at[0])
    cot_copy.start()
    gains_copy = pltpu.make_async_copy(gains_in, gains, in_sem.at[6])
    gains_copy.start()
    if group == 1:

        def fetch(j):
            x_copy(plane(j) * q + diagonal).start()
            x_copy(plane(j) * q + near_one(j)).start()

        if q > 1:
            loop(1, m + 1, fetch)
            loop(1, m + 1, lambda j: x_copy(plane(j) * q + near_two(j)).start())
        loop(1, m + 1, lambda j: x_copy(plane(j) * q + mp).start())
    else:
        loop(0, chunks, lambda c: x_copy(c).start())
    own_rows = pl.ds(pl.multiple_of(me * size, 16), size)
    local_copies = [
        pltpu.make_async_copy(next_in, rows_in, in_sem.at[1]),
        pltpu.make_async_copy(weight_in.at[own_rows], kw, in_sem.at[2]),
        pltpu.make_async_copy(master_in, master, in_sem.at[3]),
        pltpu.make_async_copy(moment_in, moment, in_sem.at[4]),
        pltpu.make_async_copy(second_in, second, in_sem.at[5]),
        pltpu.make_async_copy(gain_in_hbm.at[me], gain_in, in_sem.at[7]),
        pltpu.make_async_copy(gmaster_in, gmaster, in_sem.at[8]),
        pltpu.make_async_copy(gmoment_in, gmoment, in_sem.at[9]),
        pltpu.make_async_copy(gsecond_in, gsecond, in_sem.at[10]),
    ]
    for copy in local_copies:
        copy.start()

    my_half = pl.ds(pl.multiple_of(half * half_rows, 16), half_rows)

    def next_block(dest):
        if group == 1:
            at = pl.ds(pl.multiple_of(dest * size, 128), size)
            return next_blocks.at[my_half, at]
        return next_blocks.at[dest, my_half]

    own_block = pltpu.make_async_copy(next_block(me), hbuf.at[half, me], own_sem)
    own_block.start()

    barrier = pltpu.get_barrier_semaphore()

    def other(j):
        return lax.rem(me + j, n)

    def greet(j):
        pl.semaphore_signal(barrier, inc=1, device_id=(other(j), ten), device_id_type=MESH)

    loop(1, n, greet)
    for t in range(1, heads):
        pl.semaphore_signal(
            barrier, inc=1, device_id=(me, lax.rem(ten + t, heads)), device_id_type=MESH
        )
    pl.semaphore_wait(barrier, n - 1 + heads - 1)

    def remote(src, dst, send, recv, dev):
        return pltpu.make_async_remote_copy(
            src_ref=src, dst_ref=dst, send_sem=send, recv_sem=recv,
            device_id=dev, device_id_type=MESH,
        )

    def h_copy(j):
        return remote(
            next_block(other(j)), hbuf.at[half, me], sh.at[j], rh.at[j], (other(j), ten)
        )

    loop(1, n, lambda j: h_copy(j).start())

    cot_copy.wait()
    gains_copy.wait()
    cot_t = cot[...].astype(jnp.float32).T.astype(jnp.bfloat16)

    def product(c):
        x_copy(c).wait()
        scaled = (xbuf[c].astype(jnp.float32) * gains[c]).astype(jnp.bfloat16)
        return jnp.dot(cot_t, scaled, preferred_element_type=jnp.float32).T

    def product_all(c):
        y = product(c)
        for g in range(group):
            prod[c * group + g] = encode(y[g * size : (g + 1) * size])

    def value(block):
        return product(block) if group == 1 else decode(prod[block])

    def copy1(j, k):
        z = plane(j)
        block = (diagonal, near_one(j), near_two(j))[k]
        to = near_two(j) if k == 2 else near_one(j)
        return remote(
            prod.at[z * q + block], got1.at[k * m + z],
            s1.at[k * m + z], r1.at[k * m + z], (mz * q + to, ten),
        )

    if group > 1:
        loop(0, chunks, product_all)

    def stage1(j):
        for k, block in enumerate((diagonal, near_one(j))):
            if group == 1:
                prod[plane(j) * q + block] = encode(product(plane(j) * q + block))
            copy1(j, k).start()

    def stage1_sum(j):
        z = plane(j)
        block = z * q + near_two(j)
        mine = value(block)
        copy1(j, 0).wait_recv()
        prod[block] = encode(mine + decode(got1[z]))
        copy1(j, 2).start()

    if q > 1:
        loop(1, m + 1, stage1)
        loop(1, m + 1, stage1_sum)

    local_copies[0].wait()
    total_row = jnp.zeros((rows, 128), jnp.float32)
    depth = rows_in.shape[1]
    for at in range(0, depth, 1024):
        piece = rows_in[:, at : at + 1024].astype(jnp.float32)
        piece = piece * piece
        for lane in range(0, 1024, 128):
            total_row = total_row + piece[:, lane : lane + 128]
    inverse = lax.rsqrt(jnp.sum(total_row, axis=1, keepdims=True) / depth + rms_eps)
    square = jnp.broadcast_to(inverse, (rows, 128))
    if rows < 128:
        square = jnp.concatenate([square, jnp.zeros((128 - rows, 128), jnp.float32)], axis=0)
    inv_all[me] = square.T[0:8]

    def i_copy(j):
        return remote(inv_all.at[me], inv_all.at[me], si.at[j], ri.at[j], (other(j), ten))

    loop(1, n, lambda j: i_copy(j).start())

    def copy2(j):
        return remote(
            give2.at[j], got2.at[j], s2.at[j], r2.at[j], (plane(j) * q + mp, ten)
        )

    def plane_sum(j):
        total = value(plane(j) * q + mp)
        if q > 1:
            for k in (1, 2):
                copy1(j, k).wait_recv()
                total = total + decode(got1[k * m + plane(j)])
        return total

    def stage2(j):
        give2[j] = encode(plane_sum(j))
        copy2(j).start()

    loop(1, m, stage2)

    own_block.wait()
    loop(1, n, lambda j: h_copy(j).wait_recv())
    mate_give = remote(hbuf.at[half], hbuf.at[half], sm, rm, (me, mate))
    mate_take = remote(hbuf.at[1 - half], hbuf.at[1 - half], sm, rm, (me, mate))
    mate_give.start()

    key_grad = plane_sum(m)
    for copy in local_copies[1:]:
        copy.wait()
    kw_t = kw[...].astype(jnp.float32).T / gain_in[...]

    loop(1, n, lambda j: i_copy(j).wait_recv())
    mate_take.wait_recv()

    def rescale(s):
        column = jnp.broadcast_to(inv_all[s][0:1], (128, 128)).T[:rows, 0:1]
        for h in range(2):
            at = slice(h * half_rows, (h + 1) * half_rows)
            resc[s, at] = hbuf[h, s].astype(jnp.float32) * column[at]

    loop(0, n, rescale)

    for j in range(1, m):
        copy2(j).wait_recv()
        key_grad = key_grad + decode(got2[j])

    grad_t = key_grad.T
    gain_all[ten, 0:1] = jnp.sum(kw_t * grad_t, axis=0, keepdims=True)
    gain_all[ten, 1:2] = jnp.sum(grad_t * grad_t, axis=0, keepdims=True)

    def g_copy(t):
        dev = (me, lax.rem(ten + t, heads))
        return remote(gain_all.at[ten], gain_all.at[ten], sg.at[t], rg.at[t], dev)

    for t in range(1, heads):
        g_copy(t).start()
    for t in range(1, heads):
        g_copy(t).wait_recv()
    gain_grad = gain_all[0, 0:1]
    squares = gain_all[0, 1:2]
    for t in range(1, heads):
        gain_grad = gain_grad + gain_all[t, 0:1]
        squares = squares + gain_all[t, 1:2]
    squares = squares + gain_grad * gain_grad
    total_all[me] = jnp.broadcast_to(jnp.sum(squares, axis=1, keepdims=True), (8, 128))

    def t_copy(j):
        return remote(total_all.at[me], total_all.at[me], st.at[j], rt.at[j], (other(j), ten))

    loop(1, n, lambda j: t_copy(j).start())
    loop(1, n, lambda j: t_copy(j).wait_recv())
    total = jnp.sum(total_all[...], axis=0)
    clip = jnp.minimum(1.0, 1.0 / (jnp.sqrt(total) + 1e-06))[0:1]

    master_new, moment_new, second_new = adam_update(
        key_grad * clip, master[...], moment[...], second[...], 0.1
    )
    master_v[...] = master_new
    moment_v[...] = moment_new
    second_v[...] = second_new
    weight = master_new.astype(jnp.bfloat16)
    gain_new, gain_moment_new, gain_second_new = adam_update(
        gain_grad * clip[:, 0:1], gmaster[...], gmoment[...], gsecond[...], 0.0
    )
    gmaster_v[...] = gain_new
    gmoment_v[...] = gain_moment_new
    gsecond_v[...] = gain_second_new
    results = [
        pltpu.make_async_copy(src, dst, out_sem.at[i])
        for i, (src, dst) in enumerate([
            (master_v, master_out), (moment_v, moment_out), (second_v, second_out),
            (gmaster_v, gmaster_out), (gmoment_v, gmoment_out), (gsecond_v, gsecond_out),
        ])
    ]
    for copy in results:
        copy.start()
    gain = gain_new.astype(jnp.bfloat16).astype(jnp.float32)

    def keys(s):
        mixed = (resc[s] * gain).astype(jnp.bfloat16)
        return jnp.dot(mixed, weight, preferred_element_type=jnp.float32)

    def a_copy(j, k):
        at = (k - 1) * m + plane(j)
        return remote(
            part.at[at], got_part.at[at], sp.at[at], rp.at[at], (mz * q + peer(k), ten)
        )

    def share(j):
        for k in range(1, q):
            part[(k - 1) * m + plane(j)] = keys(plane(j) * q + peer(k))
            a_copy(j, k).start()

    loop(1, m + 1, share)

    def b_copy(j):
        dev = (plane(j) * q + mp, ten)
        return remote(give_keys.at[j], got_keys.at[j], s3.at[j], r3.at[j], dev)

    def plane_keys(j):
        total = keys(plane(j) * q + mp)
        for k in range(1, q):
            a_copy(j, k).wait_recv()
            total = total + got_part[(k - 1) * m + plane(j)]
        return total

    def pass_on(j):
        give_keys[j] = plane_keys(j)
        b_copy(j).start()

    loop(1, m, pass_on)
    keys_sum = plane_keys(m)
    for j in range(1, m):
        b_copy(j).wait_recv()
        keys_sum = keys_sum + got_keys[j]
    keys_v[...] = keys_sum.astype(jnp.bfloat16)
    keys_copy = pltpu.make_async_copy(keys_v, keys_out, out_sem.at[6])
    keys_copy.start()

    def drain(j):
        h_copy(j).wait_send()
        i_copy(j).wait_send()
        t_copy(j).wait_send()

    loop(1, n, drain)

    def drain1(j):
        for k in range(1, q):
            copy1(j, k - 1).wait_send()
            a_copy(j, k).wait_send()

    loop(1, m + 1, drain1)
    def drain2(j):
        copy2(j).wait_send()
        b_copy(j).wait_send()

    loop(1, m, drain2)
    mate_give.wait_send()
    for t in range(1, heads):
        g_copy(t).wait_send()
    for copy in results:
        copy.wait()
    keys_copy.wait()


def hand_over(*refs):
    count = 7
    given, taken, held = refs[:count], refs[count : 2 * count], refs[2 * count : 3 * count]
    sems = refs[-1]
    loads = [pltpu.make_async_copy(given[i], held[i], sems.at[i]) for i in range(count)]
    stores = [
        pltpu.make_async_copy(held[i], taken[i], sems.at[count + i]) for i in range(count)
    ]
    for copy in loads:
        copy.start()
    for load, store in zip(loads, stores):
        load.wait()
        store.start()
    for copy in stores:
        copy.wait()


def local(
    normed,
    key_cot,
    key_weight,
    norm_gain,
    weight_master,
    weight_moment,
    weight_second,
    gain_master,
    gain_moment,
    gain_second,
    next_input,
):
    n = lax.axis_size("dp")
    heads = lax.axis_size("tensor")
    tokens, depth = normed.shape
    size = depth // n
    cols = key_cot.shape[1]
    rows = next_input.shape[0]
    half_rows = rows // 2
    q = 4 if n % 4 == 0 else 1
    m = n // q
    width = size if size % 128 == 0 else 512
    group = width // size
    chunks = depth // width
    dims = (n, heads, q, m, size, width, group, chunks, rows, half_rows)
    if group == 1:
        blocks = next_input
    else:
        blocks = next_input.reshape(rows, n, size).transpose(1, 0, 2)
    gain = norm_gain.astype(jnp.float32)
    hbm = pl.BlockSpec(memory_space=pl.ANY)
    f32, bf16 = jnp.float32, jnp.bfloat16
    dma = pltpu.SemaphoreType.DMA
    shard = jax.ShapeDtypeStruct((size, cols), f32)
    line = jax.ShapeDtypeStruct((1, size), f32)
    shapes = (
        jax.ShapeDtypeStruct((rows, cols), bf16), shard, shard, shard, line, line, line,
    )
    outs = pl.pallas_call(
        functools.partial(kernel, dims),
        out_shape=shapes,
        in_specs=[hbm] * 13,
        out_specs=(hbm,) * 7,
        scratch_shapes=[
            pltpu.VMEM((chunks, tokens, width), bf16),
            pltpu.VMEM((tokens, cols), bf16),
            pltpu.VMEM((size, cols), bf16),
            pltpu.VMEM((size, cols), f32),
            pltpu.VMEM((size, cols), f32),
            pltpu.VMEM((size, cols), f32),
            pltpu.VMEM((rows, depth), bf16),
            pltpu.VMEM((n, size, cols), bf16),
            pltpu.VMEM((max(q - 1, 1) * m, size, cols), bf16),
            pltpu.VMEM((m, size, cols), bf16),
            pltpu.VMEM((m, size, cols), bf16),
            pltpu.VMEM((2, n, half_rows, size), bf16),
            pltpu.VMEM((n, rows, size), f32),
            pltpu.VMEM((n, 8, 128), f32),
            pltpu.VMEM((heads, 8, size), f32),
            pltpu.VMEM((n, 8, 128), f32),
            pltpu.VMEM((max(q - 1, 1) * m, rows, cols), f32),
            pltpu.VMEM((max(q - 1, 1) * m, rows, cols), f32),
            pltpu.VMEM((m, rows, cols), f32),
            pltpu.VMEM((m, rows, cols), f32),
            pltpu.VMEM((chunks, 1, width), f32),
            pltpu.VMEM((1, size), f32),
            pltpu.VMEM((1, size), f32),
            pltpu.VMEM((1, size), f32),
            pltpu.VMEM((1, size), f32),
            pltpu.VMEM((rows, cols), bf16),
            pltpu.VMEM((size, cols), f32),
            pltpu.VMEM((size, cols), f32),
            pltpu.VMEM((size, cols), f32),
            pltpu.VMEM((1, size), f32),
            pltpu.VMEM((1, size), f32),
            pltpu.VMEM((1, size), f32),
            dma((chunks,)), dma((11,)), dma,
            dma((max(q - 1, 1) * m,)), dma((max(q - 1, 1) * m,)),
            dma((m,)), dma((m,)),
            dma((n,)), dma((n,)),
            dma, dma,
            dma((n,)), dma((n,)),
            dma((heads,)), dma((heads,)),
            dma((n,)), dma((n,)),
            dma((max(q - 1, 1) * m,)), dma((max(q - 1, 1) * m,)),
            dma((m,)), dma((m,)), dma((7,)),
        ],
        compiler_params=pltpu.CompilerParams(
            collective_id=0, has_side_effects=True, vmem_limit_bytes=64 * 1024 * 1024
        ),
        cost_estimate=pl.CostEstimate(
            flops=2 * tokens * depth * cols + 2 * n * rows * size * cols,
            bytes_accessed=2 * tokens * depth,
            transcendentals=0,
        ),
    )(
        normed, key_cot, key_weight,
        gain.reshape(chunks, 1, width), gain.reshape(n, 1, size), weight_master, weight_moment, weight_second,
        gain_master.reshape(1, size), gain_moment.reshape(1, size),
        gain_second.reshape(1, size), next_input, blocks,
    )
    outs = pl.pallas_call(
        hand_over,
        out_shape=shapes,
        in_specs=[hbm] * 7,
        out_specs=(hbm,) * 7,
        scratch_shapes=[pltpu.VMEM(o.shape, o.dtype) for o in shapes] + [dma((14,))],
        compiler_params=pltpu.CompilerParams(vmem_limit_bytes=64 * 1024 * 1024),
    )(*outs)
    keys, master, moment, second, gmaster, gmoment, gsecond = outs
    return (
        keys, master, moment, second,
        gmaster.reshape(size), gmoment.reshape(size), gsecond.reshape(size),
    )


def solution(mesh):
    return jax.shard_map(
        local,
        mesh=mesh,
        in_specs=(
            P("dp", None),
            P("dp", "tensor"),
            P(None, "tensor"),
            P(),
            P("dp", "tensor"),
            P("dp", "tensor"),
            P("dp", "tensor"),
            P("dp"),
            P("dp"),
            P("dp"),
            P("dp", None),
        ),
        out_specs=(
            P("dp", "tensor"),
            P("dp", "tensor"),
            P("dp", "tensor"),
            P("dp", "tensor"),
            P("dp"),
            P("dp"),
            P("dp"),
        ),
        check_vma=False,
    )
```

```python
import functools

import jax
import jax.numpy as jnp
from jax import lax
from jax.experimental import pallas as pl
from jax.experimental.pallas import tpu as pltpu
from jax.sharding import PartitionSpec as P

beta_one = 0.9
beta_two = 0.95
adam_eps = 1e-08
learn_rate = 0.001
rms_eps = 1e-05
step_count = 10
MESH = pl.DeviceIdType.MESH


def adam_update(grad, master, moment, second, decay):
    moment_new = beta_one * moment + (1.0 - beta_one) * grad
    second_new = beta_two * second + (1.0 - beta_two) * grad * grad
    corr_one = 1.0 - beta_one**step_count
    corr_two = 1.0 - beta_two**step_count
    update = moment_new / corr_one / (jnp.sqrt(second_new / corr_two) + adam_eps) + decay * master
    return (master - learn_rate * update, moment_new, second_new)


def encode(value):
    return (value * jnp.abs(value) * (value * value)).astype(jnp.bfloat16)


def decode(coded):
    power = coded.astype(jnp.float32)
    size = jnp.maximum(jnp.abs(power), 1.2e-38)
    root = lax.rsqrt(size)
    return power * root * lax.rsqrt(size * root)


def kernel(
    dims,
    normed, cot_in, weight_in, gains_in, gain_in_hbm, master_in, moment_in, second_in,
    gmaster_in, gmoment_in, gsecond_in, next_in, next_blocks,
    keys_out, master_out, moment_out, second_out, gmaster_out, gmoment_out, gsecond_out,
    xbuf, cot, kw, master, moment, second, rows_in, prod, got1, give2, got2,
    hbuf, resc, inv_all, gain_all, total_all, part, got_part, give_keys, got_keys,
    gains, gain_in, gmaster, gmoment, gsecond, keys_v, master_v, moment_v, second_v,
    gmaster_v, gmoment_v, gsecond_v, gains_raw,
    x_sem, in_sem, own_sem, s1, r1, s2, r2, sh, rh, sm, rm, si, ri, sg, rg, st, rt, sp, rp, s3, r3, out_sem,
):
    n, heads, q, m, size, width, group, chunks, rows, half_rows = dims
    me = lax.axis_index("dp")
    ten = lax.axis_index("tensor")
    mp = lax.rem(me, q)
    mz = lax.div(me, q)
    half = lax.rem(ten, 2)
    mate = ten + 1 - 2 * half

    def x_copy(c):
        at = pl.ds(pl.multiple_of(c * width, 128), width)
        return pltpu.make_async_copy(normed.at[:, at], xbuf.at[c], x_sem.at[c])

    def loop(low, high, body):
        def step(i, carry):
            body(i)
            return carry

        lax.fori_loop(low, high, step, 0)

    def peer(k):
        return lax.rem(mp + k, q)

    def plane(j):
        return lax.rem(mz + j, m)

    across = lax.rem(mp, 2)
    along = lax.div(mp, 2)
    in_row = 1 - across + 2 * along
    in_column = across + 2 * (1 - along)
    diagonal = 3 - mp

    def near_one(j):
        return in_column + (in_row - in_column) * lax.rem(j, 2)

    def near_two(j):
        return in_row + (in_column - in_row) * lax.rem(j, 2)

    cot_copy = pltpu.make_async_copy(cot_in, cot, in_sem.at[0])
    cot_copy.start()
    gains_copy = pltpu.make_async_copy(
        gains_in, gains_raw if group == 1 else gains, in_sem.at[6]
    )
    gains_copy.start()
    if group == 1:

        def fetch(j):
            x_copy(plane(j) * q + diagonal).start()
            x_copy(plane(j) * q + near_one(j)).start()

        if q > 1:
            loop(1, m + 1, fetch)
            loop(1, m + 1, lambda j: x_copy(plane(j) * q + near_two(j)).start())
        loop(1, m + 1, lambda j: x_copy(plane(j) * q + mp).start())
    else:
        loop(0, chunks, lambda c: x_copy(c).start())
    own_rows = pl.ds(pl.multiple_of(me * size, 16), size)
    local_copies = [
        pltpu.make_async_copy(next_in, rows_in, in_sem.at[1]),
        pltpu.make_async_copy(weight_in.at[own_rows], kw, in_sem.at[2]),
        pltpu.make_async_copy(master_in, master, in_sem.at[3]),
        pltpu.make_async_copy(moment_in, moment, in_sem.at[4]),
        pltpu.make_async_copy(second_in, second, in_sem.at[5]),
        pltpu.make_async_copy(gmaster_in, gmaster, in_sem.at[8]),
        pltpu.make_async_copy(gmoment_in, gmoment, in_sem.at[9]),
        pltpu.make_async_copy(gsecond_in, gsecond, in_sem.at[10]),
    ]
    if group > 1:
        local_copies.append(
            pltpu.make_async_copy(gain_in_hbm.at[me], gain_in, in_sem.at[7])
        )
    for copy in local_copies:
        copy.start()

    my_half = pl.ds(pl.multiple_of(half * half_rows, 16), half_rows)

    def next_block(dest):
        if group == 1:
            at = pl.ds(pl.multiple_of(dest * size, 128), size)
            return next_blocks.at[my_half, at]
        return next_blocks.at[dest, my_half]

    own_block = pltpu.make_async_copy(next_block(me), hbuf.at[half, me], own_sem)
    own_block.start()

    barrier = pltpu.get_barrier_semaphore()

    def other(j):
        return lax.rem(me + j, n)

    def greet(j):
        pl.semaphore_signal(barrier, inc=1, device_id=(other(j), ten), device_id_type=MESH)

    loop(1, n, greet)
    for t in range(1, heads):
        pl.semaphore_signal(
            barrier, inc=1, device_id=(me, lax.rem(ten + t, heads)), device_id_type=MESH
        )
    pl.semaphore_wait(barrier, n - 1 + heads - 1)

    def remote(src, dst, send, recv, dev):
        return pltpu.make_async_remote_copy(
            src_ref=src, dst_ref=dst, send_sem=send, recv_sem=recv,
            device_id=dev, device_id_type=MESH,
        )

    def h_copy(j):
        return remote(
            next_block(other(j)), hbuf.at[half, me], sh.at[j], rh.at[j], (other(j), ten)
        )

    def h_plane(j):
        for k in range(1 if j is m else 0, q):
            h_copy(lax.rem(plane(j) * q + peer(k) - me + n, n)).start()


    cot_copy.wait()
    gains_copy.wait()
    if group == 1:
        for c in range(chunks):
            gains[c, 0] = gains_raw[c * width : (c + 1) * width].astype(jnp.float32)
    cot_t = cot[...].astype(jnp.float32).T.astype(jnp.bfloat16)

    def product(c):
        x_copy(c).wait()
        scaled = (xbuf[c].astype(jnp.float32) * gains[c]).astype(jnp.bfloat16)
        return jnp.dot(cot_t, scaled, preferred_element_type=jnp.float32).T

    def product_all(c):
        y = product(c)
        for g in range(group):
            prod[c * group + g] = encode(y[g * size : (g + 1) * size])

    def value(block):
        return product(block) if group == 1 else decode(prod[block])

    def copy1(j, k):
        z = plane(j)
        block = (diagonal, near_one(j), near_two(j))[k]
        to = near_two(j) if k == 2 else near_one(j)
        return remote(
            prod.at[z * q + block], got1.at[k * m + z],
            s1.at[k * m + z], r1.at[k * m + z], (mz * q + to, ten),
        )

    if group > 1:
        loop(0, chunks, product_all)

    def stage1(j):
        for k, block in enumerate((diagonal, near_one(j))):
            if group == 1:
                prod[plane(j) * q + block] = encode(product(plane(j) * q + block))
            copy1(j, k).start()

    def stage1_sum(j):
        z = plane(j)
        block = z * q + near_two(j)
        mine = value(block)
        copy1(j, 0).wait_recv()
        prod[block] = encode(mine + decode(got1[z]))
        copy1(j, 2).start()

    def stage1_send(j):
        if q > 1:
            stage1(j)
        h_plane(j)

    loop(1, m, stage1_send)
    stage1_send(m)
    if q > 1:
        loop(1, m + 1, stage1_sum)

    local_copies[0].wait()
    total_row = jnp.zeros((rows, 128), jnp.float32)
    depth = rows_in.shape[1]
    for at in range(0, depth, 1024):
        piece = rows_in[:, at : at + 1024].astype(jnp.float32)
        piece = piece * piece
        for lane in range(0, 1024, 128):
            total_row = total_row + piece[:, lane : lane + 128]
    inverse = lax.rsqrt(jnp.sum(total_row, axis=1, keepdims=True) / depth + rms_eps)
    square = jnp.broadcast_to(inverse, (rows, 128))
    if rows < 128:
        square = jnp.concatenate([square, jnp.zeros((128 - rows, 128), jnp.float32)], axis=0)
    inv_all[me] = square.T[0:8]

    def i_copy(j):
        return remote(inv_all.at[me], inv_all.at[me], si.at[j], ri.at[j], (other(j), ten))

    loop(1, n, lambda j: i_copy(j).start())

    def copy2(j):
        return remote(
            give2.at[j], got2.at[j], s2.at[j], r2.at[j], (plane(j) * q + mp, ten)
        )

    def plane_sum(j):
        total = value(plane(j) * q + mp)
        if q > 1:
            for k in (1, 2):
                copy1(j, k).wait_recv()
                total = total + decode(got1[k * m + plane(j)])
        return total

    def stage2(j):
        give2[j] = encode(plane_sum(j))
        copy2(j).start()

    loop(1, m, stage2)

    own_block.wait()
    loop(1, n, lambda j: h_copy(j).wait_recv())
    mate_give = remote(hbuf.at[half], hbuf.at[half], sm, rm, (me, mate))
    mate_take = remote(hbuf.at[1 - half], hbuf.at[1 - half], sm, rm, (me, mate))
    mate_give.start()

    key_grad = plane_sum(m)
    for copy in local_copies[1:]:
        copy.wait()
    kw_t = kw[...].astype(jnp.float32).T / (gains[me] if group == 1 else gain_in[...])

    loop(1, n, lambda j: i_copy(j).wait_recv())
    mate_take.wait_recv()

    def rescale(s):
        column = jnp.broadcast_to(inv_all[s][0:1], (128, 128)).T[:rows, 0:1]
        for h in range(2):
            at = slice(h * half_rows, (h + 1) * half_rows)
            resc[s, at] = hbuf[h, s].astype(jnp.float32) * column[at]

    loop(0, n, rescale)

    for j in range(1, m):
        copy2(j).wait_recv()
        key_grad = key_grad + decode(got2[j])

    grad_t = key_grad.T
    gain_all[ten, 0:1] = jnp.sum(kw_t * grad_t, axis=0, keepdims=True)
    gain_all[ten, 1:2] = jnp.sum(grad_t * grad_t, axis=0, keepdims=True)

    def g_copy(t):
        dev = (me, lax.rem(ten + t, heads))
        return remote(gain_all.at[ten], gain_all.at[ten], sg.at[t], rg.at[t], dev)

    for t in range(1, heads):
        g_copy(t).start()
    for t in range(1, heads):
        g_copy(t).wait_recv()
    gain_grad = gain_all[0, 0:1]
    squares = gain_all[0, 1:2]
    for t in range(1, heads):
        gain_grad = gain_grad + gain_all[t, 0:1]
        squares = squares + gain_all[t, 1:2]
    squares = squares + gain_grad * gain_grad
    total_all[me] = jnp.broadcast_to(jnp.sum(squares, axis=1, keepdims=True), (8, 128))

    def t_copy(j):
        return remote(total_all.at[me], total_all.at[me], st.at[j], rt.at[j], (other(j), ten))

    loop(1, n, lambda j: t_copy(j).start())
    loop(1, n, lambda j: t_copy(j).wait_recv())
    total = jnp.sum(total_all[...], axis=0)
    clip = jnp.minimum(1.0, 1.0 / (jnp.sqrt(total) + 1e-06))[0:1]

    master_new, moment_new, second_new = adam_update(
        key_grad * clip, master[...], moment[...], second[...], 0.1
    )
    master_v[...] = master_new
    moment_v[...] = moment_new
    second_v[...] = second_new
    weight = master_new.astype(jnp.bfloat16)
    gain_new, gain_moment_new, gain_second_new = adam_update(
        gain_grad * clip[:, 0:1], gmaster[...], gmoment[...], gsecond[...], 0.0
    )
    gmaster_v[...] = gain_new
    gmoment_v[...] = gain_moment_new
    gsecond_v[...] = gain_second_new
    results = [
        pltpu.make_async_copy(src, dst, out_sem.at[i])
        for i, (src, dst) in enumerate([
            (master_v, master_out), (moment_v, moment_out), (second_v, second_out),
            (gmaster_v, gmaster_out), (gmoment_v, gmoment_out), (gsecond_v, gsecond_out),
        ])
    ]
    for copy in results:
        copy.start()
    gain = gain_new.astype(jnp.bfloat16).astype(jnp.float32)

    def keys(z):
        mixed = (resc[pl.ds(z * q, q)] * gain).astype(jnp.bfloat16).reshape(q * rows, size)
        made = jnp.dot(mixed, weight, preferred_element_type=jnp.float32)
        part[pl.ds(z * q, q)] = made.reshape(q, rows, -1)

    def a_copy(j, k):
        at = (k - 1) * m + plane(j)
        return remote(
            part.at[plane(j) * q + peer(k)], got_part.at[at], sp.at[at], rp.at[at], (mz * q + peer(k), ten)
        )

    def share(j):
        keys(plane(j))
        for k in range(1, q):
            a_copy(j, k).start()

    loop(1, m + 1, share)

    def b_copy(j):
        dev = (plane(j) * q + mp, ten)
        return remote(give_keys.at[j], got_keys.at[j], s3.at[j], r3.at[j], dev)

    def plane_keys(j):
        total = part[plane(j) * q + mp]
        for k in range(1, q):
            a_copy(j, k).wait_recv()
            total = total + got_part[(k - 1) * m + plane(j)]
        return total

    def pass_on(j):
        give_keys[j] = plane_keys(j)
        b_copy(j).start()

    loop(1, m, pass_on)
    keys_sum = plane_keys(m)
    for j in range(1, m):
        b_copy(j).wait_recv()
        keys_sum = keys_sum + got_keys[j]
    keys_v[...] = keys_sum.astype(jnp.bfloat16)
    keys_copy = pltpu.make_async_copy(keys_v, keys_out, out_sem.at[6])
    keys_copy.start()

    def drain(j):
        h_copy(j).wait_send()
        i_copy(j).wait_send()
        t_copy(j).wait_send()

    loop(1, n, drain)

    def drain1(j):
        for k in range(1, q):
            copy1(j, k - 1).wait_send()
            a_copy(j, k).wait_send()

    loop(1, m + 1, drain1)
    def drain2(j):
        copy2(j).wait_send()
        b_copy(j).wait_send()

    loop(1, m, drain2)
    mate_give.wait_send()
    for t in range(1, heads):
        g_copy(t).wait_send()
    for copy in results:
        copy.wait()
    keys_copy.wait()


def hand_over(*refs):
    count = 7
    given, taken, held = refs[:count], refs[count : 2 * count], refs[2 * count : 3 * count]
    sems = refs[-1]
    loads = [pltpu.make_async_copy(given[i], held[i], sems.at[i]) for i in range(count)]
    stores = [
        pltpu.make_async_copy(held[i], taken[i], sems.at[count + i]) for i in range(count)
    ]
    for copy in loads:
        copy.start()
    for load, store in zip(loads, stores):
        load.wait()
        store.start()
    for copy in stores:
        copy.wait()


def local(
    normed,
    key_cot,
    key_weight,
    norm_gain,
    weight_master,
    weight_moment,
    weight_second,
    gain_master,
    gain_moment,
    gain_second,
    next_input,
):
    n = lax.axis_size("dp")
    heads = lax.axis_size("tensor")
    tokens, depth = normed.shape
    size = depth // n
    cols = key_cot.shape[1]
    rows = next_input.shape[0]
    half_rows = rows // 2
    q = 4 if n % 4 == 0 else 1
    m = n // q
    width = size if size % 128 == 0 else 512
    group = width // size
    chunks = depth // width
    dims = (n, heads, q, m, size, width, group, chunks, rows, half_rows)
    if group == 1:
        blocks = next_input
    else:
        blocks = next_input.reshape(rows, n, size).transpose(1, 0, 2)
    if group == 1:
        gains = own_gains = norm_gain
    else:
        gain = norm_gain.astype(jnp.float32)
        gains, own_gains = gain.reshape(chunks, 1, width), gain.reshape(n, 1, size)
    hbm = pl.BlockSpec(memory_space=pl.ANY)
    f32, bf16 = jnp.float32, jnp.bfloat16
    dma = pltpu.SemaphoreType.DMA
    shard = jax.ShapeDtypeStruct((size, cols), f32)
    line = jax.ShapeDtypeStruct((1, size), f32)
    shapes = (
        jax.ShapeDtypeStruct((rows, cols), bf16), shard, shard, shard, line, line, line,
    )
    outs = pl.pallas_call(
        functools.partial(kernel, dims),
        out_shape=shapes,
        in_specs=[hbm] * 13,
        out_specs=(hbm,) * 7,
        scratch_shapes=[
            pltpu.VMEM((chunks, tokens, width), bf16),
            pltpu.VMEM((tokens, cols), bf16),
            pltpu.VMEM((size, cols), bf16),
            pltpu.VMEM((size, cols), f32),
            pltpu.VMEM((size, cols), f32),
            pltpu.VMEM((size, cols), f32),
            pltpu.VMEM((rows, depth), bf16),
            pltpu.VMEM((n, size, cols), bf16),
            pltpu.VMEM((max(q - 1, 1) * m, size, cols), bf16),
            pltpu.VMEM((m, size, cols), bf16),
            pltpu.VMEM((m, size, cols), bf16),
            pltpu.VMEM((2, n, half_rows, size), bf16),
            pltpu.VMEM((n, rows, size), f32),
            pltpu.VMEM((n, 8, 128), f32),
            pltpu.VMEM((heads, 8, size), f32),
            pltpu.VMEM((n, 8, 128), f32),
            pltpu.VMEM((n, rows, cols), f32),
            pltpu.VMEM((max(q - 1, 1) * m, rows, cols), f32),
            pltpu.VMEM((m, rows, cols), f32),
            pltpu.VMEM((m, rows, cols), f32),
            pltpu.VMEM((chunks, 1, width), f32),
            pltpu.VMEM((1, size), f32),
            pltpu.VMEM((1, size), f32),
            pltpu.VMEM((1, size), f32),
            pltpu.VMEM((1, size), f32),
            pltpu.VMEM((rows, cols), bf16),
            pltpu.VMEM((size, cols), f32),
            pltpu.VMEM((size, cols), f32),
            pltpu.VMEM((size, cols), f32),
            pltpu.VMEM((1, size), f32),
            pltpu.VMEM((1, size), f32),
            pltpu.VMEM((1, size), f32),
            pltpu.VMEM((depth,), bf16),
            dma((chunks,)), dma((11,)), dma,
            dma((max(q - 1, 1) * m,)), dma((max(q - 1, 1) * m,)),
            dma((m,)), dma((m,)),
            dma((n,)), dma((n,)),
            dma, dma,
            dma((n,)), dma((n,)),
            dma((heads,)), dma((heads,)),
            dma((n,)), dma((n,)),
            dma((max(q - 1, 1) * m,)), dma((max(q - 1, 1) * m,)),
            dma((m,)), dma((m,)), dma((7,)),
        ],
        compiler_params=pltpu.CompilerParams(
            collective_id=0, has_side_effects=True, vmem_limit_bytes=64 * 1024 * 1024
        ),
        cost_estimate=pl.CostEstimate(
            flops=2 * tokens * depth * cols + 2 * n * rows * size * cols,
            bytes_accessed=2 * tokens * depth,
            transcendentals=0,
        ),
    )(
        normed, key_cot, key_weight,
        gains, own_gains, weight_master, weight_moment, weight_second,
        gain_master.reshape(1, size), gain_moment.reshape(1, size),
        gain_second.reshape(1, size), next_input, blocks,
    )
    outs = pl.pallas_call(
        hand_over,
        out_shape=shapes,
        in_specs=[hbm] * 7,
        out_specs=(hbm,) * 7,
        scratch_shapes=[pltpu.VMEM(o.shape, o.dtype) for o in shapes] + [dma((14,))],
        compiler_params=pltpu.CompilerParams(vmem_limit_bytes=64 * 1024 * 1024),
    )(*outs)
    keys, master, moment, second, gmaster, gmoment, gsecond = outs
    return (
        keys, master, moment, second,
        gmaster.reshape(size), gmoment.reshape(size), gsecond.reshape(size),
    )


def solution(mesh):
    return jax.shard_map(
        local,
        mesh=mesh,
        in_specs=(
            P("dp", None),
            P("dp", "tensor"),
            P(None, "tensor"),
            P(),
            P("dp", "tensor"),
            P("dp", "tensor"),
            P("dp", "tensor"),
            P("dp"),
            P("dp"),
            P("dp"),
            P("dp", None),
        ),
        out_specs=(
            P("dp", "tensor"),
            P("dp", "tensor"),
            P("dp", "tensor"),
            P("dp", "tensor"),
            P("dp"),
            P("dp"),
            P("dp"),
        ),
        check_vma=False,
    )
```
